32 devices in a mesh: width: 4 (over y, x), store: 8 (over z, core).
Axes of the slice: x: 2, y: 2, z: 4, core: 2. Of those that a mesh axis runs over, the one named last changes fastest.
Arguments:
- activations: bfloat16 [64, 512, 8192], P('store', None, 'width'), may hold values from -6 to 6
- out_grads: bfloat16 [64, 512, 8192], P('store', None, 'width'), may hold values from -6 to 6
- proj_in: bfloat16 [8192, 64], P('width'), may hold values from -0.0625 to 0.0625
- proj_out: bfloat16 [8192, 64], P('width'), may hold values from -0.0625 to 0.0625
- fisher_inv: float32 [4096, 4096], P('store', 'width'), may hold values from -0.09375 to 0.09375
- grad_store: float32 [16384, 4096], P('store', 'width'), may hold values from -6 to 6
Outputs:
- scores: float32 [64, 16384], P('width', 'store')
The draws below stay inside these ranges and needn't reach their ends.
All inputs are finite; a program needn't handle non-finite values.
Results may differ from the reference program's by a relative error of at most 0.0003.
Values sent between devices are 32-bit elements; how exact they have to be, the bound alone decides.
A program may use at most 128 MiB of HBM per device.

```python
import jax
import jax.numpy as jnp
from jax import lax

D = 8192
RANK = 64
SEQ = 512
COORD = 4096
QUERIES = 64
EXAMPLES = 16384


def block_levels(stream_key, extent, cuts, smallest, largest):
    level, own = 1.0, jax.random.fold_in(stream_key, 6)
    for dim, blocks in cuts:
        steps = jnp.exp(jax.random.uniform(jax.random.fold_in(own, dim), (blocks,), jnp.float32, smallest / len(cuts), largest / len(cuts)))
        level = level * jnp.repeat(steps, extent[dim] // blocks).reshape([-1 if axis == dim else 1 for axis in range(len(extent))])
    return level


def centred(stream_key, extent, scale, limit, shards=(), held_as=jnp.bfloat16):
    loudness = block_levels(stream_key, extent, shards, -0.22, 0.18) if shards else 1.0
    values = jax.random.normal(stream_key, extent, jnp.float32) * scale * loudness
    return jnp.minimum(jnp.maximum(values, -limit), limit).astype(held_as)


def setup_inputs(seed: int = 0) -> dict:
    streams_of = jax.random.split(jax.random.key(seed), 7)
    activations = centred(streams_of[0], (QUERIES, SEQ, D), 1.0, 6.0, ((0, 8), (2, 4)))
    out_grads = centred(streams_of[1], (QUERIES, SEQ, D), 1.0, 6.0, ((0, 8), (2, 4)))
    proj_in = centred(streams_of[2], (D, RANK), D ** -0.5, 0.0625, ((0, 4),))
    proj_out = centred(streams_of[3], (D, RANK), D ** -0.5, 0.0625, ((0, 4),))
    fisher_inv = centred(streams_of[4], (COORD, COORD), COORD ** -0.5, 0.09375, ((0, 8), (1, 4)), jnp.float32)
    grad_store = centred(streams_of[5], (EXAMPLES, COORD), 1.0, 6.0, ((0, 8), (1, 4)), jnp.float32)
    return dict(activations=activations, out_grads=out_grads, proj_in=proj_in, proj_out=proj_out, fisher_inv=fisher_inv, grad_store=grad_store)


def reference(activations, out_grads, proj_in, proj_out, fisher_inv, grad_store):
    queries = activations.shape[0]
    act_proj = jnp.dot(activations.reshape(-1, D), proj_in, preferred_element_type=jnp.float32).reshape(queries, SEQ, RANK)
    grad_proj = jnp.dot(out_grads.reshape(-1, D), proj_out, preferred_element_type=jnp.float32).reshape(queries, SEQ, RANK)
    gradient = jnp.einsum("qti,qtj->qij", grad_proj, act_proj, precision=lax.Precision.HIGHEST) / SEQ
    gradient = gradient.reshape(queries, COORD)
    precond = jnp.dot(gradient, fisher_inv, precision=lax.Precision.HIGHEST)
    return jnp.dot(precond, grad_store.T, precision=lax.Precision.HIGHEST)
```

```python
import functools

import jax
import jax.numpy as jnp
from jax import lax
from jax.experimental import pallas as pl
from jax.experimental.pallas import tpu as pltpu
from jax.sharding import PartitionSpec as P

DEPTH = 4
COLS = 4
LANES = 128
F32, BF16 = jnp.float32, jnp.bfloat16


def split(value):
    high = value.astype(BF16)
    return high, (value - high.astype(F32)).astype(BF16)


def dot(a, b, dims=((1,), (0,))):
    return lax.dot_general(a, b, (dims, ((), ())), preferred_element_type=F32)


def plan(tall, per):
    first_x = [(dy, 1, p, 0) for dy in list(range(1, tall)) + [0] for p in range(per)]
    first_y = [(dy, dx, p, 1) for dx in (1, 0) for dy in range(1, tall) for p in range(per)]
    one = []
    for i in range(max(len(first_x), len(first_y))):
        one += first_x[i : i + 1] + first_y[i : i + 1]
    two = [(dy, 0, p, 0) for dy in range(1, tall) for p in range(per)] + [(0, 1, p, 1) for p in range(per)]
    own = [(0, 0, p, h) for p in range(per) for h in range(2)]
    return one, two, own


def pick(k, values):
    found = jnp.int32(values[0])
    for i, value in enumerate(values[1:]):
        found = jnp.where(k == i + 1, jnp.int32(value), found)
    return found


def kernel(dims, act, grd, pin, pout, fis, sto, out, abuf, gbuf, win, wout, held, recv1, recv2, sraw, shi, slo, fraw,
           fhi, flo, gsend, graw, pp, prs, pred, pfull, scb, rsc, lsem, bsem, s1, r1, s2, r2, sa, ra, sb, rb, sr, rr, sg,
           rg, sc, rc):
    wide, stores, per, seq, rank = dims
    tall, half, count = wide // 2, seq // 2, wide * stores
    w, s = lax.axis_index("width"), lax.axis_index("store")
    y, x = w // 2, w % 2
    one, two, own = plan(tall, per)
    chunks = one + two + own
    place = {c: i for i, c in enumerate(chunks)}
    n1 = len(one)

    def remote(src, dst, send, recv, axis, index):
        return pltpu.make_async_remote_copy(src_ref=src, dst_ref=dst, send_sem=send, recv_sem=recv,
                                            device_id={axis: index}, device_id_type=pl.DeviceIdType.MESH)

    def owner_of(k):
        dy, dx, p, h = (pick(k, [c[i] for c in chunks]) for i in range(4))
        return dy, dx, p, h

    def loads(k):
        dy, dx, p, h = owner_of(k)
        owner = ((y + dy) % tall) * 2 + (x + dx) % 2
        rows = pl.ds(pl.multiple_of((owner * per + p) * seq + h * half, half), half)
        slot = k % DEPTH
        return (pltpu.make_async_copy(grd.at[rows, :], gbuf.at[slot], bsem.at[0, slot]),
                pltpu.make_async_copy(act.at[rows, :], abuf.at[slot], bsem.at[1, slot]))

    for k in range(DEPTH):
        for load in loads(jnp.int32(k)):
            load.start()

    barrier = pltpu.get_barrier_semaphore()
    for axis, me, size in (("width", w, wide), ("store", s, stores)):
        for d in range(1, size):
            pl.semaphore_signal(barrier, inc=1, device_id={axis: (me + d) % size}, device_id_type=pl.DeviceIdType.MESH)

    blank = jnp.zeros(pin.shape, BF16)
    wout[...] = jnp.concatenate([pout[...], blank], axis=1)
    win[...] = jnp.concatenate([blank, pin[...]], axis=1)
    pl.semaphore_wait(barrier, wide + stores - 2)

    def project(k, carry):
        for load in loads(k):
            load.wait()
        slot = k % DEPTH
        held[k] = dot(gbuf[slot], wout[...]) + dot(abuf[slot], win[...])

        @pl.when(k < n1)
        def _():
            dy, dx, p, h = owner_of(k)
            target = ((y + dy * h) % tall) * 2 + (x + 1 - h) % 2
            remote(held.at[k], recv1.at[k], s1.at[k], r1.at[k], "width", target).start()

        @pl.when(k + DEPTH < len(chunks))
        def _():
            for load in loads(k + DEPTH):
                load.start()

        return carry

    lax.fori_loop(0, len(chunks), project, 0)

    load_f = pltpu.make_async_copy(fis, fraw, lsem.at[0])
    load_s = pltpu.make_async_copy(sto, sraw, lsem.at[1])
    load_f.start()
    load_s.start()

    def got1(c):
        k = place[c]
        remote(held.at[k], recv1.at[k], s1.at[k], r1.at[k], "width", w).wait_recv()
        return recv1[k]

    def got2(c):
        k = place[c] - n1
        remote(held.at[k + n1], recv2.at[k], s2.at[k], r2.at[k], "width", w).wait_recv()
        return recv2[k]

    for c in two:
        dy, dx, p, h = c
        k = place[c]
        total = held[k]
        for other in ([(dy, 1, p, 0)] if h == 0 else [(e, 1, p, 1) for e in range(1, tall)]):
            total = total + got1(other)
        held[k] = total
        target = ((y + dy) % tall) * 2 + (x + dx) % 2
        remote(held.at[k], recv2.at[k - n1], s2.at[k - n1], r2.at[k - n1], "width", target).start()

    load_f.wait()
    fhi[...], flo[...] = split(fraw[...])
    load_s.wait()
    step = sto.shape[0] // 16

    def split_store(i, carry):
        rows = pl.ds(pl.multiple_of(i * step, step), step)
        shi[rows, :], slo[rows, :] = split(sraw[rows, :])
        return carry

    lax.fori_loop(0, 16, split_store, 0)

    lane = lax.broadcasted_iota(jnp.int32, (rank, LANES), 1)
    packed = jnp.zeros((rank, LANES), F32)
    for p in range(per):
        top = held[place[0, 0, p, 0]] + got1((0, 1, p, 0))
        low = held[place[0, 0, p, 1]] + got2((0, 1, p, 1))
        for dy in range(1, tall):
            top = top + got2((dy, 0, p, 0))
            low = low + got1((dy, 0, p, 1))
        both = jnp.concatenate(split(jnp.concatenate([top, low], axis=0)), axis=1)
        outer = dot(both, both, ((0,), (0,)))
        mean = (outer[:rank, :LANES] + outer[:rank, LANES:] + outer[LANES : LANES + rank, :LANES]) * (1.0 / seq)
        if p == 0:
            packed = jnp.where(lane < rank, pltpu.roll(mean, rank, 1), packed)
        else:
            packed = jnp.where(lane >= rank, mean, packed)
    rows_i = rank // stores
    gsend[...] = packed.reshape(stores, rows_i, LANES)

    def ship_a(d):
        peer = (s + d) % stores
        return remote(gsend.at[peer], graw.at[s, w], sa.at[d], ra.at[d], "store", peer)

    for d in range(1, stores):
        ship_a(d).start()
    graw[s, w] = gsend[s]
    for d in range(1, stores):
        ship_a(d).wait_recv()

    def ship_b(d):
        return remote(graw.at[:, w], graw.at[:, w], sb.at[d], rb.at[d], "width", (w + d) % wide)

    for d in range(1, wide):
        ship_b(d).start()
    for d in range(1, wide):
        ship_b(d).wait_recv()

    got = graw[...].reshape(count, rows_i, LANES)
    lane = lax.broadcasted_iota(jnp.int32, (count, LANES), 1)
    sides = [[] for _ in range(per)]
    for i in range(0, rows_i, 2):
        even, odd = got[:, i, :], got[:, i + 1, :]
        sides[0].append(jnp.where(lane < rank, even, pltpu.roll(odd, rank, 1)))
        if per == 2:
            sides[1].append(jnp.where(lane < rank, pltpu.roll(even, rank, 1), odd))
    left = jnp.concatenate([jnp.concatenate(side, axis=1) for side in sides], axis=0)
    queries = per * count
    lhi, llo = split(left)
    two_rows = dot(jnp.concatenate([lhi, llo], axis=0), fhi[...])
    partial = two_rows[:queries] + two_rows[queries:] + dot(lhi, flo[...])
    pp[...] = partial.reshape(pp.shape)

    def ship_r(d):
        peer = (s + d) % stores
        return remote(pp.at[peer], prs.at[d], sr.at[d], rr.at[d], "store", peer)

    for d in range(1, stores):
        ship_r(d).start()
    total = pp[s]
    for d in range(1, stores):
        ship_r(d).wait_recv()
        total = total + prs[d]
    pred[...] = total

    def ship_g(d):
        return remote(pred, pfull.at[s], sg.at[d], rg.at[d], "store", (s + d) % stores)

    for d in range(1, stores):
        ship_g(d).start()
    pfull[s] = total
    for d in range(1, stores):
        ship_g(d).wait_recv()

    precond = pfull[...].reshape(queries, pfull.shape[2])
    phi, plo = split(precond)
    stacked = jnp.concatenate([phi, plo], axis=0)
    span = sto.shape[0] // COLS

    def ship_c(c, d):
        peer = (w + d) % wide
        return remote(scb.at[c, peer], rsc.at[c, d], sc.at[c, d], rc.at[c, d], "width", peer)

    for c in range(COLS):
        rows = pl.ds(c * span, span)
        wide_rows = dot(stacked, shi[rows, :], ((1,), (1,)))
        score = wide_rows[:queries] + wide_rows[queries:] + dot(phi, slo[rows, :], ((1,), (1,)))
        for r in range(wide):
            for p in range(per):
                at = p * count + r * stores
                scb[c, r, p * stores : (p + 1) * stores, :] = score[at : at + stores]
        for d in range(1, wide):
            ship_c(c, d).start()
    for c in range(COLS):
        total = scb[c, w]
        for d in range(1, wide):
            ship_c(c, d).wait_recv()
            total = total + rsc[c, d]
        out[:, c * span : (c + 1) * span] = total

    for k in range(n1):
        remote(held.at[k], recv1.at[k], s1.at[k], r1.at[k], "width", w).wait_send()
    for k in range(len(two)):
        remote(held.at[k + n1], recv2.at[k], s2.at[k], r2.at[k], "width", w).wait_send()
    for d in range(1, stores):
        ship_a(d).wait_send()
        ship_r(d).wait_send()
        ship_g(d).wait_send()
    for d in range(1, wide):
        ship_b(d).wait_send()
        for c in range(COLS):
            ship_c(c, d).wait_send()


def body(wide, stores, activations, out_grads, proj_in, proj_out, fisher_inv, grad_store):
    group, seq, width = activations.shape
    rank = proj_in.shape[1]
    per = group // wide
    half = seq // 2
    one, two, own = plan(wide // 2, per)
    examples, coords = grad_store.shape
    queries = group * stores
    block, out_rows = queries // stores, queries // wide
    rows_i = rank // stores
    span = examples // COLS
    dma = pltpu.SemaphoreType.DMA
    flat = (group * seq, width)
    n1, n2 = len(one), len(two)
    result = pl.pallas_call(
        functools.partial(kernel, (wide, stores, per, seq, rank)),
        out_shape=jax.ShapeDtypeStruct((out_rows, examples), F32),
        in_specs=[pl.BlockSpec(memory_space=pl.ANY)] * 2
        + [pl.BlockSpec(memory_space=pltpu.VMEM)] * 2
        + [pl.BlockSpec(memory_space=pl.ANY)] * 2,
        out_specs=pl.BlockSpec(memory_space=pltpu.VMEM),
        scratch_shapes=[
            pltpu.VMEM((DEPTH, half, width), BF16),
            pltpu.VMEM((DEPTH, half, width), BF16),
            pltpu.VMEM((width, LANES), BF16),
            pltpu.VMEM((width, LANES), BF16),
            pltpu.VMEM((n1 + n2 + len(own), half, LANES), F32),
            pltpu.VMEM((n1, half, LANES), F32),
            pltpu.VMEM((n2, half, LANES), F32),
            pltpu.VMEM(grad_store.shape, F32),
            pltpu.VMEM(grad_store.shape, BF16),
            pltpu.VMEM(grad_store.shape, BF16),
            pltpu.VMEM(fisher_inv.shape, F32),
            pltpu.VMEM(fisher_inv.shape, BF16),
            pltpu.VMEM(fisher_inv.shape, BF16),
            pltpu.VMEM((stores, rows_i, LANES), F32),
            pltpu.VMEM((stores, wide, rows_i, LANES), F32),
            pltpu.VMEM((stores, block, coords), F32),
            pltpu.VMEM((stores, block, coords), F32),
            pltpu.VMEM((block, coords), F32),
            pltpu.VMEM((stores, block, coords), F32),
            pltpu.VMEM((COLS, wide, out_rows, span), F32),
            pltpu.VMEM((COLS, wide, out_rows, span), F32),
            dma((2,)),
            dma((2, DEPTH)),
            dma((n1,)),
            dma((n1,)),
            dma((n2,)),
            dma((n2,)),
            dma((stores,)),
            dma((stores,)),
            dma((wide,)),
            dma((wide,)),
            dma((stores,)),
            dma((stores,)),
            dma((stores,)),
            dma((stores,)),
            dma((COLS, wide)),
            dma((COLS, wide)),
        ],
        compiler_params=pltpu.CompilerParams(collective_id=0, has_side_effects=True, vmem_limit_bytes=56 * 2**20),
        name="influence",
    )(activations.reshape(flat), out_grads.reshape(flat), proj_in, proj_out, fisher_inv, grad_store)
    return result.reshape(per, out_rows // per, examples).transpose(1, 0, 2).reshape(out_rows, examples)


def solution(mesh):
    placed = (
        P("store", None, "width"),
        P("store", None, "width"),
        P("width", None),
        P("width", None),
        P("store", "width"),
        P("store", "width"),
    )
    return jax.shard_map(
        functools.partial(body, mesh.shape["width"], mesh.shape["store"]),
        mesh=mesh, in_specs=placed, out_specs=P("width", "store"), check_vma=False,
    )
```

```python
import functools

import jax
import jax.numpy as jnp
from jax import lax
from jax.experimental import pallas as pl
from jax.experimental.pallas import tpu as pltpu
from jax.sharding import PartitionSpec as P

DEPTH = 4
COLS = 4
LANES = 128
F32, BF16 = jnp.float32, jnp.bfloat16


def split(value):
    high = value.astype(BF16)
    return high, (value - high.astype(F32)).astype(BF16)


def dot(a, b, dims=((1,), (0,))):
    return lax.dot_general(a, b, (dims, ((), ())), preferred_element_type=F32)


def plan(tall, p):
    first_x = [(dy, 1, p, 0) for dy in list(range(1, tall)) + [0]]
    first_y = [(dy, dx, p, 1) for dx in (1, 0) for dy in range(1, tall)]
    one = []
    for i in range(max(len(first_x), len(first_y))):
        one += first_x[i : i + 1] + first_y[i : i + 1]
    two = [(dy, 0, p, 0) for dy in range(1, tall)] + [(0, 1, p, 1)]
    own = [(0, 0, p, h) for h in range(2)]
    return one, two, own


def pick(k, values):
    found = jnp.int32(values[0])
    for i, value in enumerate(values[1:]):
        found = jnp.where(k == i + 1, jnp.int32(value), found)
    return found


def kernel(dims, act, grd, pin, pout, fis, sto, out, abuf, gbuf, win, wout, held, recv1, recv2, sraw, shi, slo, fraw,
           fhi, flo, gsend, graw, pp, prs, pred, pfull, scb, rsc, lsem, bsem, s1, r1, s2, r2, sa, ra, sb, rb, sr, rr, sg,
           rg, sc, rc):
    wide, stores, per, seq, rank = dims
    tall, half, count = wide // 2, seq // 2, wide * stores
    w, s = lax.axis_index("width"), lax.axis_index("store")
    y, x = w // 2, w % 2
    plans = [plan(tall, p) for p in range(per)]
    chunks = [c for p in range(per) for group in plans[p] for c in group]
    place = {c: i for i, c in enumerate(chunks)}
    n1, n2 = len(plans[0][0]), len(plans[0][1])
    each = len(chunks) // per

    def remote(src, dst, send, recv, axis, index):
        return pltpu.make_async_remote_copy(src_ref=src, dst_ref=dst, send_sem=send, recv_sem=recv,
                                            device_id={axis: index}, device_id_type=pl.DeviceIdType.MESH)

    def owner_of(k):
        return [pick(k, [c[i] for c in chunks]) for i in range(4)]

    def loads(k):
        dy, dx, p, h = owner_of(k)
        owner = ((y + dy) % tall) * 2 + (x + dx) % 2
        rows = pl.ds(pl.multiple_of((owner * per + p) * seq + h * half, half), half)
        slot = k % DEPTH
        return (pltpu.make_async_copy(grd.at[rows, :], gbuf.at[slot], bsem.at[0, slot]),
                pltpu.make_async_copy(act.at[rows, :], abuf.at[slot], bsem.at[1, slot]))

    for k in range(DEPTH):
        for load in loads(jnp.int32(k)):
            load.start()

    barrier = pltpu.get_barrier_semaphore()
    for axis, me, size in (("width", w, wide), ("store", s, stores)):
        for d in range(1, size):
            pl.semaphore_signal(barrier, inc=1, device_id={axis: (me + d) % size}, device_id_type=pl.DeviceIdType.MESH)

    blank = jnp.zeros(pin.shape, BF16)
    wout[...] = jnp.concatenate([pout[...], blank], axis=0).T
    win[...] = jnp.concatenate([blank, pin[...]], axis=0).T
    pl.semaphore_wait(barrier, wide + stores - 2)

    def project(k, carry):
        for load in loads(k):
            load.wait()
        slot = k % DEPTH
        held[k] = dot(gbuf[slot], wout[...]) + dot(abuf[slot], win[...])

        @pl.when(k % each < n1)
        def _():
            dy, dx, p, h = owner_of(k)
            target = ((y + dy * h) % tall) * 2 + (x + 1 - h) % 2
            at = (k // each) * n1 + k % each
            remote(held.at[k], recv1.at[at], s1.at[at], r1.at[at], "width", target).start()

        @pl.when(k + DEPTH < len(chunks))
        def _():
            for load in loads(k + DEPTH):
                load.start()

        return carry

    def ship_1(c):
        k = place[c]
        at = c[2] * n1 + k % each
        return remote(held.at[k], recv1.at[at], s1.at[at], r1.at[at], "width", w), at

    def ship_2(c):
        k = place[c]
        at = c[2] * n2 + k % each - n1
        target = ((y + c[0]) % tall) * 2 + (x + c[1]) % 2
        return remote(held.at[k], recv2.at[at], s2.at[at], r2.at[at], "width", target), at

    def got1(c):
        copy, at = ship_1(c)
        copy.wait_recv()
        return recv1[at]

    def got2(c):
        copy, at = ship_2(c)
        copy.wait_recv()
        return recv2[at]

    def forward(p):
        for c in plans[p][1]:
            dy, dx, _, h = c
            total = held[place[c]]
            for other in ([(dy, 1, p, 0)] if h == 0 else [(e, 1, p, 1) for e in range(1, tall)]):
                total = total + got1(other)
            held[place[c]] = total
            ship_2(c)[0].start()

    rows_i = rank // stores

    def ship_a(p, d):
        peer = (s + d) % stores
        return remote(gsend.at[p, peer], graw.at[p, s, w], sa.at[p, d], ra.at[p, d], "store", peer)

    def ship_b(p, d):
        return remote(graw.at[p, :, w], graw.at[p, :, w], sb.at[p, d], rb.at[p, d], "width", (w + d) % wide)

    def gradient(p):
        top = held[place[0, 0, p, 0]] + got1((0, 1, p, 0))
        low = held[place[0, 0, p, 1]] + got2((0, 1, p, 1))
        for dy in range(1, tall):
            top = top + got2((dy, 0, p, 0))
            low = low + got1((dy, 0, p, 1))
        both = jnp.concatenate(split(jnp.concatenate([top, low], axis=0)), axis=1)
        outer = dot(both, both, ((0,), (0,)))
        mean = (outer[:rank, :LANES] + outer[:rank, LANES:] + outer[LANES : LANES + rank, :LANES]) * (1.0 / seq)
        gsend[p] = mean.reshape(stores, rows_i, LANES)
        for d in range(1, stores):
            ship_a(p, d).start()
        graw[p, s, w] = gsend[p, s]

    def gather(p):
        for d in range(1, stores):
            ship_a(p, d).wait_recv()
        for d in range(1, wide):
            ship_b(p, d).start()

    by_rows = count % (8 * stores) == 0
    block, coords = pp.shape[2], pp.shape[3]

    def ship_r(p, d):
        peer = (s + d) % stores
        return remote(pp.at[p, peer], prs.at[p, d], sr.at[p, d], rr.at[p, d], "store", peer)

    def ship_g(p, d):
        return remote(pred.at[p], pfull.at[p, s], sg.at[p, d], rg.at[p, d], "store", (s + d) % stores)

    def condition(p):
        for d in range(1, wide):
            ship_b(p, d).wait_recv()
        got = graw[p].reshape(count, rows_i, LANES)
        lane = lax.broadcasted_iota(jnp.int32, (count, LANES), 1)
        pairs = [jnp.where(lane < rank, pltpu.roll(got[:, i, :], rank, 1), got[:, i + 1, :]) for i in range(0, rows_i, 2)]
        left = jnp.concatenate(split(jnp.concatenate(pairs, axis=1)), axis=0)
        double = dot(left, fhi[...]) + dot(left, flo[...])
        partial = double[:count] + double[count:]
        for r in range(stores):
            if by_rows:
                pp[p, r] = partial[r * block : (r + 1) * block]
            else:
                pp[p, r] = partial[:, r * coords : (r + 1) * coords]
        for d in range(1, stores):
            ship_r(p, d).start()

    def combine(p):
        total = pp[p, s]
        for d in range(1, stores):
            ship_r(p, d).wait_recv()
            total = total + prs[p, d]
        pred[p] = total
        pfull[p, s] = total
        for d in range(1, stores):
            ship_g(p, d).start()

    span = sto.shape[0] // COLS

    def ship_c(p, c, d):
        peer = (w + d) % wide
        return remote(scb.at[p, c, peer], rsc.at[p, c, d], sc.at[p, c, d], rc.at[p, c, d], "width", peer)

    def score(p):
        for d in range(1, stores):
            ship_g(p, d).wait_recv()
        precond = jnp.concatenate([pfull[p, r] for r in range(stores)], axis=0 if by_rows else 1)
        stacked = jnp.concatenate(split(precond), axis=0)
        for c in range(COLS):
            rows = pl.ds(c * span, span)
            double = dot(shi[rows, :], stacked, ((1,), (1,))) + dot(slo[rows, :], stacked, ((1,), (1,)))
            double = double.T
            scores = double[:count] + double[count:]
            for r in range(wide):
                scb[p, c, r] = scores[r * stores : (r + 1) * stores]
            for d in range(1, wide):
                ship_c(p, c, d).start()

    def finish(p):
        for c in range(COLS):
            total = scb[p, c, w]
            for d in range(1, wide):
                ship_c(p, c, d).wait_recv()
                total = total + rsc[p, c, d]
            out[p * stores : (p + 1) * stores, c * span : (c + 1) * span] = total

    load_f = pltpu.make_async_copy(fis, fraw, lsem.at[0])
    load_s = pltpu.make_async_copy(sto, sraw, lsem.at[1])

    def split_fisher():
        load_f.wait()
        fhi[...], flo[...] = split(fraw[...])

    def split_store():
        load_s.wait()
        step = sto.shape[0] // 16

        def part(i, carry):
            rows = pl.ds(pl.multiple_of(i * step, step), step)
            shi[rows, :], slo[rows, :] = split(sraw[rows, :])
            return carry

        lax.fori_loop(0, 16, part, 0)

    for p in range(per):
        if p == per - 1:
            load_f.start()
        lax.fori_loop(p * each, (p + 1) * each, project, 0)
        if p + 1 < per:
            forward(p)
    load_s.start()
    split_fisher()
    if per == 2:
        gradient(0)
        gather(0)
        forward(1)
        condition(0)
        split_store()
        gradient(1)
        combine(0)
        gather(1)
        condition(1)
        score(0)
        combine(1)
        score(1)
    else:
        forward(per - 1)
        split_store()
        for p in range(per):
            gradient(p)
            gather(p)
            condition(p)
            combine(p)
            score(p)
    for p in range(per):
        finish(p)

    for p in range(per):
        for c in plans[p][0]:
            ship_1(c)[0].wait_send()
        for c in plans[p][1]:
            ship_2(c)[0].wait_send()
        for d in range(1, stores):
            ship_a(p, d).wait_send()
            ship_r(p, d).wait_send()
            ship_g(p, d).wait_send()
        for d in range(1, wide):
            ship_b(p, d).wait_send()
            for c in range(COLS):
                ship_c(p, c, d).wait_send()


def body(wide, stores, activations, out_grads, proj_in, proj_out, fisher_inv, grad_store):
    group, seq, width = activations.shape
    rank = proj_in.shape[1]
    per = group // wide
    half = seq // 2
    one, two, own = plan(wide // 2, 0)
    n1, n2 = len(one), len(two)
    examples, coords = grad_store.shape
    count = wide * stores
    queries = per * count
    out_rows = queries // wide
    if count % (8 * stores) == 0:
        piece = (count // stores, coords)
    else:
        piece = (count, coords // stores)
    rows_i = rank // stores
    span = examples // COLS
    dma = pltpu.SemaphoreType.DMA
    flat = (group * seq, width)
    result = pl.pallas_call(
        functools.partial(kernel, (wide, stores, per, seq, rank)),
        out_shape=jax.ShapeDtypeStruct((out_rows, examples), F32),
        in_specs=[pl.BlockSpec(memory_space=pl.ANY)] * 2
        + [pl.BlockSpec(memory_space=pltpu.VMEM)] * 2
        + [pl.BlockSpec(memory_space=pl.ANY)] * 2,
        out_specs=pl.BlockSpec(memory_space=pltpu.VMEM),
        scratch_shapes=[
            pltpu.VMEM((DEPTH, half, width), BF16),
            pltpu.VMEM((DEPTH, half, width), BF16),
            pltpu.VMEM((width, LANES), BF16),
            pltpu.VMEM((width, LANES), BF16),
            pltpu.VMEM((per * (n1 + n2 + len(own)), half, LANES), F32),
            pltpu.VMEM((per * n1, half, LANES), F32),
            pltpu.VMEM((per * n2, half, LANES), F32),
            pltpu.VMEM(grad_store.shape, F32),
            pltpu.VMEM(grad_store.shape, BF16),
            pltpu.VMEM(grad_store.shape, BF16),
            pltpu.VMEM(fisher_inv.shape, F32),
            pltpu.VMEM(fisher_inv.shape, BF16),
            pltpu.VMEM(fisher_inv.shape, BF16),
            pltpu.VMEM((per, stores, rows_i, LANES), F32),
            pltpu.VMEM((per, stores, wide, rows_i, LANES), F32),
            pltpu.VMEM((per, stores, *piece), F32),
            pltpu.VMEM((per, stores, *piece), F32),
            pltpu.VMEM((per, *piece), F32),
            pltpu.VMEM((per, stores, *piece), F32),
            pltpu.VMEM((per, COLS, wide, stores, span), F32),
            pltpu.VMEM((per, COLS, wide, stores, span), F32),
            dma((2,)),
            dma((2, DEPTH)),
            dma((per * n1,)),
            dma((per * n1,)),
            dma((per * n2,)),
            dma((per * n2,)),
            dma((per, stores)),
            dma((per, stores)),
            dma((per, wide)),
            dma((per, wide)),
            dma((per, stores)),
            dma((per, stores)),
            dma((per, stores)),
            dma((per, stores)),
            dma((per, COLS, wide)),
            dma((per, COLS, wide)),
        ],
        compiler_params=pltpu.CompilerParams(collective_id=0, has_side_effects=True, vmem_limit_bytes=56 * 2**20),
        name="influence",
    )(activations.reshape(flat), out_grads.reshape(flat), proj_in.T, proj_out.T, fisher_inv, grad_store)
    return result.reshape(per, out_rows // per, examples).transpose(1, 0, 2).reshape(out_rows, examples)


def solution(mesh):
    placed = (
        P("store", None, "width"),
        P("store", None, "width"),
        P("width", None),
        P("width", None),
        P("store", "width"),
        P("store", "width"),
    )
    return jax.shard_map(
        functools.partial(body, mesh.shape["width"], mesh.shape["store"]),
        mesh=mesh, in_specs=placed, out_specs=P("width", "store"), check_vma=False,
    )
```

```python
import functools

import jax
import jax.numpy as jnp
from jax import lax
from jax.experimental import pallas as pl
from jax.experimental.pallas import tpu as pltpu
from jax.sharding import PartitionSpec as P

DEPTH = 4
COLS = 4
LANES = 128
F32, BF16 = jnp.float32, jnp.bfloat16


def split(value):
    high = value.astype(BF16)
    return high, (value - high.astype(F32)).astype(BF16)


def dot(a, b, dims=((1,), (0,))):
    return lax.dot_general(a, b, (dims, ((), ())), preferred_element_type=F32)


def plan(tall, p):
    first_x = [(dy, 1, p, 0) for dy in list(range(1, tall)) + [0]]
    first_y = [(dy, dx, p, 1) for dx in (1, 0) for dy in range(1, tall)]
    one = []
    for i in range(max(len(first_x), len(first_y))):
        one += first_x[i : i + 1] + first_y[i : i + 1]
    two = [(dy, 0, p, 0) for dy in range(1, tall)] + [(0, 1, p, 1)]
    own = [(0, 0, p, h) for h in range(2)]
    return one, two, own


def pick(k, values):
    found = jnp.int32(values[0])
    for i, value in enumerate(values[1:]):
        found = jnp.where(k == i + 1, jnp.int32(value), found)
    return found


def kernel(dims, act, grd, pin, pout, fis, sto, out, abuf, gbuf, win, wout, held, recv1, recv2, sraw, shi, slo, fraw,
           fhi, flo, gsend, graw, pp, prs, pred, pfull, scb, rsc, lsem, bsem, s1, r1, s2, r2, sa, ra, sb, rb, sr, rr, sg,
           rg, sc, rc):
    wide, stores, per, seq, rank = dims
    tall, half, count = wide // 2, seq // 2, wide * stores
    w, s = lax.axis_index("width"), lax.axis_index("store")
    y, x = w // 2, w % 2
    plans = [plan(tall, p) for p in range(per)]
    chunks = [c for p in range(per) for group in plans[p] for c in group]
    place = {c: i for i, c in enumerate(chunks)}
    n1, n2 = len(plans[0][0]), len(plans[0][1])
    each = len(chunks) // per

    def remote(src, dst, send, recv, axis, index):
        return pltpu.make_async_remote_copy(src_ref=src, dst_ref=dst, send_sem=send, recv_sem=recv,
                                            device_id={axis: index}, device_id_type=pl.DeviceIdType.MESH)

    def owner_of(k):
        return [pick(k, [c[i] for c in chunks]) for i in range(4)]

    def loads(k):
        dy, dx, p, h = owner_of(k)
        owner = ((y + dy) % tall) * 2 + (x + dx) % 2
        rows = pl.ds(pl.multiple_of((owner * per + p) * seq + h * half, half), half)
        slot = k % DEPTH
        return (pltpu.make_async_copy(grd.at[rows, :], gbuf.at[slot], bsem.at[0, slot]),
                pltpu.make_async_copy(act.at[rows, :], abuf.at[slot], bsem.at[1, slot]))

    for k in range(DEPTH):
        for load in loads(jnp.int32(k)):
            load.start()

    barrier = pltpu.get_barrier_semaphore()
    for axis, me, size in (("width", w, wide), ("store", s, stores)):
        for d in range(1, size):
            pl.semaphore_signal(barrier, inc=1, device_id={axis: (me + d) % size}, device_id_type=pl.DeviceIdType.MESH)

    blank = jnp.zeros(pin.shape, BF16)
    wout[...] = jnp.concatenate([pout[...], blank], axis=0).T
    win[...] = jnp.concatenate([blank, pin[...]], axis=0).T
    pl.semaphore_wait(barrier, wide + stores - 2)

    def project(k, carry):
        for load in loads(k):
            load.wait()
        slot = k % DEPTH
        held[k] = dot(gbuf[slot], wout[...]) + dot(abuf[slot], win[...])

        @pl.when(k % each < n1)
        def _():
            dy, dx, p, h = owner_of(k)
            target = ((y + dy * h) % tall) * 2 + (x + 1 - h) % 2
            at = (k // each) * n1 + k % each
            remote(held.at[k], recv1.at[at], s1.at[at], r1.at[at], "width", target).start()

        @pl.when(k + DEPTH < len(chunks))
        def _():
            for load in loads(k + DEPTH):
                load.start()

        return carry

    def ship_1(c):
        k = place[c]
        at = c[2] * n1 + k % each
        return remote(held.at[k], recv1.at[at], s1.at[at], r1.at[at], "width", w), at

    def ship_2(c):
        k = place[c]
        at = c[2] * n2 + k % each - n1
        target = ((y + c[0]) % tall) * 2 + (x + c[1]) % 2
        return remote(held.at[k], recv2.at[at], s2.at[at], r2.at[at], "width", target), at

    def got1(c):
        copy, at = ship_1(c)
        copy.wait_recv()
        return recv1[at]

    def got2(c):
        copy, at = ship_2(c)
        copy.wait_recv()
        return recv2[at]

    def forward(p):
        for c in plans[p][1]:
            dy, dx, _, h = c
            total = held[place[c]]
            for other in ([(dy, 1, p, 0)] if h == 0 else [(e, 1, p, 1) for e in range(1, tall)]):
                total = total + got1(other)
            held[place[c]] = total
            ship_2(c)[0].start()

    rows_i = rank // stores

    def ship_a(p, d):
        peer = (s + d) % stores
        return remote(gsend.at[p, peer], graw.at[p, s, w], sa.at[p, d], ra.at[p, d], "store", peer)

    def ship_b(p, d):
        return remote(graw.at[p, :, w], graw.at[p, :, w], sb.at[p, d], rb.at[p, d], "width", (w + d) % wide)

    def gradient(p):
        top = held[place[0, 0, p, 0]] + got1((0, 1, p, 0))
        low = held[place[0, 0, p, 1]] + got2((0, 1, p, 1))
        for dy in range(1, tall):
            top = top + got2((dy, 0, p, 0))
            low = low + got1((dy, 0, p, 1))
        both = jnp.concatenate(split(jnp.concatenate([top, low], axis=0)), axis=1)
        outer = dot(both, both, ((0,), (0,)))
        mean = (outer[:rank, :LANES] + outer[:rank, LANES:] + outer[LANES : LANES + rank, :LANES]) * (1.0 / seq)
        gsend[p] = mean.reshape(stores, rows_i, LANES)
        for d in range(1, stores):
            ship_a(p, d).start()
        graw[p, s, w] = gsend[p, s]

    def gather(p):
        for d in range(1, stores):
            ship_a(p, d).wait_recv()
        for d in range(1, wide):
            ship_b(p, d).start()

    by_rows = count % (8 * stores) == 0
    block, coords = pp.shape[2], pp.shape[3]

    def ship_r(p, d):
        peer = (s + d) % stores
        return remote(pp.at[p, peer], prs.at[p, d], sr.at[p, d], rr.at[p, d], "store", peer)

    def ship_g(p, d):
        return remote(pred.at[p], pfull.at[p, s], sg.at[p, d], rg.at[p, d], "store", (s + d) % stores)

    def condition(p):
        for d in range(1, wide):
            ship_b(p, d).wait_recv()
        got = graw[p].reshape(count, rows_i, LANES)
        lane = lax.broadcasted_iota(jnp.int32, (count, LANES), 1)
        pairs = [jnp.where(lane < rank, pltpu.roll(got[:, i, :], rank, 1), got[:, i + 1, :]) for i in range(0, rows_i, 2)]
        left = jnp.concatenate(split(jnp.concatenate(pairs, axis=1)), axis=0)
        double = dot(left, fhi[...]) + dot(left, flo[...])
        partial = double[:count] + double[count:]
        for r in range(stores):
            if by_rows:
                pp[p, r] = partial[r * block : (r + 1) * block]
            else:
                pp[p, r] = partial[:, r * coords : (r + 1) * coords]
        for d in range(1, stores):
            ship_r(p, d).start()

    def combine(p):
        total = pp[p, s]
        for d in range(1, stores):
            ship_r(p, d).wait_recv()
            total = total + prs[p, d]
        pred[p] = total
        pfull[p, s] = total
        for d in range(1, stores):
            ship_g(p, d).start()

    span = sto.shape[0] // COLS

    def ship_c(p, c, d):
        peer = (w + d) % wide
        return remote(scb.at[p, c, peer], rsc.at[p, c, d], sc.at[p, c, d], rc.at[p, c, d], "width", peer)

    def score(p):
        for d in range(1, stores):
            ship_g(p, d).wait_recv()
        precond = jnp.concatenate([pfull[p, r] for r in range(stores)], axis=0 if by_rows else 1)
        stacked = jnp.concatenate(split(precond), axis=0)
        for c in range(COLS):
            rows = pl.ds(c * span, span)
            double = dot(shi[rows, :], stacked, ((1,), (1,))) + dot(slo[rows, :], stacked, ((1,), (1,)))
            double = double.T
            scores = double[:count] + double[count:]
            for r in range(wide):
                scb[p, c, r] = scores[r * stores : (r + 1) * stores]
            for d in range(1, wide):
                ship_c(p, c, d).start()

    def finish(p):
        for c in range(COLS):
            total = scb[p, c, w]
            for d in range(1, wide):
                ship_c(p, c, d).wait_recv()
                total = total + rsc[p, c, d]
            out[p * stores : (p + 1) * stores, c * span : (c + 1) * span] = total

    load_f = pltpu.make_async_copy(fis, fraw, lsem.at[0])
    load_s = pltpu.make_async_copy(sto, sraw, lsem.at[1])

    def split_fisher():
        load_f.wait()
        fhi[...], flo[...] = split(fraw[...])

    def split_store():
        load_s.wait()
        step = sto.shape[0] // 16

        def part(i, carry):
            rows = pl.ds(pl.multiple_of(i * step, step), step)
            shi[rows, :], slo[rows, :] = split(sraw[rows, :])
            return carry

        lax.fori_loop(0, 16, part, 0)

    late = (per - 1) * each + n1
    lax.fori_loop(0, late, project, 0)
    load_f.start()
    for p in range(per - 1):
        forward(p)
    lax.fori_loop(late, per * each, project, 0)
    load_s.start()
    split_fisher()
    if per == 2:
        forward(1)
        gradient(0)
        split_store()
        gather(0)
        gradient(1)
        condition(0)
        gather(1)
        combine(0)
        condition(1)
        score(0)
        combine(1)
        score(1)
    else:
        forward(per - 1)
        split_store()
        for p in range(per):
            gradient(p)
            gather(p)
            condition(p)
            combine(p)
            score(p)
    for p in range(per):
        finish(p)

    for p in range(per):
        for c in plans[p][0]:
            ship_1(c)[0].wait_send()
        for c in plans[p][1]:
            ship_2(c)[0].wait_send()
        for d in range(1, stores):
            ship_a(p, d).wait_send()
            ship_r(p, d).wait_send()
            ship_g(p, d).wait_send()
        for d in range(1, wide):
            ship_b(p, d).wait_send()
            for c in range(COLS):
                ship_c(p, c, d).wait_send()


def body(wide, stores, activations, out_grads, proj_in, proj_out, fisher_inv, grad_store):
    group, seq, width = activations.shape
    rank = proj_in.shape[1]
    per = group // wide
    half = seq // 2
    one, two, own = plan(wide // 2, 0)
    n1, n2 = len(one), len(two)
    examples, coords = grad_store.shape
    count = wide * stores
    queries = per * count
    out_rows = queries // wide
    if count % (8 * stores) == 0:
        piece = (count // stores, coords)
    else:
        piece = (count, coords // stores)
    rows_i = rank // stores
    span = examples // COLS
    dma = pltpu.SemaphoreType.DMA
    flat = (group * seq, width)
    result = pl.pallas_call(
        functools.partial(kernel, (wide, stores, per, seq, rank)),
        out_shape=jax.ShapeDtypeStruct((out_rows, examples), F32),
        in_specs=[pl.BlockSpec(memory_space=pl.ANY)] * 2
        + [pl.BlockSpec(memory_space=pltpu.VMEM)] * 2
        + [pl.BlockSpec(memory_space=pl.ANY)] * 2,
        out_specs=pl.BlockSpec(memory_space=pltpu.VMEM),
        scratch_shapes=[
            pltpu.VMEM((DEPTH, half, width), BF16),
            pltpu.VMEM((DEPTH, half, width), BF16),
            pltpu.VMEM((width, LANES), BF16),
            pltpu.VMEM((width, LANES), BF16),
            pltpu.VMEM((per * (n1 + n2 + len(own)), half, LANES), F32),
            pltpu.VMEM((per * n1, half, LANES), F32),
            pltpu.VMEM((per * n2, half, LANES), F32),
            pltpu.VMEM(grad_store.shape, F32),
            pltpu.VMEM(grad_store.shape, BF16),
            pltpu.VMEM(grad_store.shape, BF16),
            pltpu.VMEM(fisher_inv.shape, F32),
            pltpu.VMEM(fisher_inv.shape, BF16),
            pltpu.VMEM(fisher_inv.shape, BF16),
            pltpu.VMEM((per, stores, rows_i, LANES), F32),
            pltpu.VMEM((per, stores, wide, rows_i, LANES), F32),
            pltpu.VMEM((per, stores, *piece), F32),
            pltpu.VMEM((per, stores, *piece), F32),
            pltpu.VMEM((per, *piece), F32),
            pltpu.VMEM((per, stores, *piece), F32),
            pltpu.VMEM((per, COLS, wide, stores, span), F32),
            pltpu.VMEM((per, COLS, wide, stores, span), F32),
            dma((2,)),
            dma((2, DEPTH)),
            dma((per * n1,)),
            dma((per * n1,)),
            dma((per * n2,)),
            dma((per * n2,)),
            dma((per, stores)),
            dma((per, stores)),
            dma((per, wide)),
            dma((per, wide)),
            dma((per, stores)),
            dma((per, stores)),
            dma((per, stores)),
            dma((per, stores)),
            dma((per, COLS, wide)),
            dma((per, COLS, wide)),
        ],
        compiler_params=pltpu.CompilerParams(collective_id=0, has_side_effects=True, vmem_limit_bytes=56 * 2**20),
        name="influence",
    )(activations.reshape(flat), out_grads.reshape(flat), proj_in.T, proj_out.T, fisher_inv, grad_store)
    return result.reshape(per, out_rows // per, examples).transpose(1, 0, 2).reshape(out_rows, examples)


def solution(mesh):
    placed = (
        P("store", None, "width"),
        P("store", None, "width"),
        P("width", None),
        P("width", None),
        P("store", "width"),
        P("store", "width"),
    )
    return jax.shard_map(
        functools.partial(body, mesh.shape["width"], mesh.shape["store"]),
        mesh=mesh, in_specs=placed, out_specs=P("width", "store"), check_vma=False,
    )
```

```python
import functools

import jax
import jax.numpy as jnp
from jax import lax
from jax.experimental import pallas as pl
from jax.experimental.pallas import tpu as pltpu
from jax.sharding import PartitionSpec as P

DEPTH = 4
COLS = 4
LANES = 128
F32, BF16 = jnp.float32, jnp.bfloat16


def split(value):
    high = value.astype(BF16)
    return high, (value - high.astype(F32)).astype(BF16)


def dot(a, b, dims=((1,), (0,))):
    return lax.dot_general(a, b, (dims, ((), ())), preferred_element_type=F32)


def plan(tall, p):
    first_x = [(dy, 1, p, 0) for dy in list(range(1, tall)) + [0]]
    first_y = [(dy, dx, p, 1) for dx in (1, 0) for dy in range(1, tall)]
    one = []
    for i in range(max(len(first_x), len(first_y))):
        one += first_x[i : i + 1] + first_y[i : i + 1]
    two = [(dy, 0, p, 0) for dy in range(1, tall)] + [(0, 1, p, 1)]
    own = [(0, 0, p, h) for h in range(2)]
    return one, two, own


def pick(k, values):
    found = jnp.int32(values[0])
    for i, value in enumerate(values[1:]):
        found = jnp.where(k == i + 1, jnp.int32(value), found)
    return found


def kernel(dims, act, grd, pin, pout, fis, sto, out, abuf, gbuf, win, wout, held, recv1, recv2, sraw, shi, slo, fraw,
           fhi, flo, gsend, graw, pp, prs, pred, pfull, scb, rsc, lsem, bsem, s1, r1, s2, r2, sa, ra, sb, rb, sr, rr, sg,
           rg, sc, rc):
    wide, stores, per, seq, rank = dims
    tall, half, count = wide // 2, seq // 2, wide * stores
    w, s = lax.axis_index("width"), lax.axis_index("store")
    y, x = w // 2, w % 2
    plans = [plan(tall, p) for p in range(per)]
    chunks = [c for p in range(per) for group in plans[p] for c in group]
    place = {c: i for i, c in enumerate(chunks)}
    n1, n2 = len(plans[0][0]), len(plans[0][1])
    each = len(chunks) // per

    def remote(src, dst, send, recv, axis, index):
        return pltpu.make_async_remote_copy(src_ref=src, dst_ref=dst, send_sem=send, recv_sem=recv,
                                            device_id={axis: index}, device_id_type=pl.DeviceIdType.MESH)

    def owner_of(k):
        return [pick(k, [c[i] for c in chunks]) for i in range(4)]

    def loads(k):
        dy, dx, p, h = owner_of(k)
        owner = ((y + dy) % tall) * 2 + (x + dx) % 2
        rows = pl.ds(pl.multiple_of((owner * per + p) * seq + h * half, half), half)
        slot = k % DEPTH
        return (pltpu.make_async_copy(grd.at[rows, :], gbuf.at[slot], bsem.at[0, slot]),
                pltpu.make_async_copy(act.at[rows, :], abuf.at[slot], bsem.at[1, slot]))

    for k in range(DEPTH):
        for load in loads(jnp.int32(k)):
            load.start()

    barrier = pltpu.get_barrier_semaphore()
    for axis, me, size in (("width", w, wide), ("store", s, stores)):
        for d in range(1, size):
            pl.semaphore_signal(barrier, inc=1, device_id={axis: (me + d) % size}, device_id_type=pl.DeviceIdType.MESH)

    blank = jnp.zeros(pin.shape, BF16)
    wout[...] = jnp.concatenate([pout[...], blank], axis=0).T
    win[...] = jnp.concatenate([blank, pin[...]], axis=0).T
    pl.semaphore_wait(barrier, wide + stores - 2)

    def project(k, carry):
        for load in loads(k):
            load.wait()
        slot = k % DEPTH
        held[k] = dot(gbuf[slot], wout[...]) + dot(abuf[slot], win[...])

        @pl.when(k % each < n1)
        def _():
            dy, dx, p, h = owner_of(k)
            target = ((y + dy * h) % tall) * 2 + (x + 1 - h) % 2
            at = (k // each) * n1 + k % each
            remote(held.at[k], recv1.at[at], s1.at[at], r1.at[at], "width", target).start()

        @pl.when(k + DEPTH < len(chunks))
        def _():
            for load in loads(k + DEPTH):
                load.start()

        return carry

    def ship_1(c):
        k = place[c]
        at = c[2] * n1 + k % each
        return remote(held.at[k], recv1.at[at], s1.at[at], r1.at[at], "width", w), at

    def ship_2(c):
        k = place[c]
        at = c[2] * n2 + k % each - n1
        target = ((y + c[0]) % tall) * 2 + (x + c[1]) % 2
        return remote(held.at[k], recv2.at[at], s2.at[at], r2.at[at], "width", target), at

    def got1(c):
        copy, at = ship_1(c)
        copy.wait_recv()
        return recv1[at]

    def got2(c):
        copy, at = ship_2(c)
        copy.wait_recv()
        return recv2[at]

    def forward(p):
        for c in plans[p][1]:
            dy, dx, _, h = c
            total = held[place[c]]
            for other in ([(dy, 1, p, 0)] if h == 0 else [(e, 1, p, 1) for e in range(1, tall)]):
                total = total + got1(other)
            held[place[c]] = total
            ship_2(c)[0].start()

    rows_i = rank // stores

    def ship_a(p, d):
        peer = (s + d) % stores
        return remote(gsend.at[p, peer], graw.at[p, s, w], sa.at[p, d], ra.at[p, d], "store", peer)

    def ship_b(p, d):
        return remote(graw.at[p, :, w], graw.at[p, :, w], sb.at[p, d], rb.at[p, d], "width", (w + d) % wide)

    def gradient(p):
        top = held[place[0, 0, p, 0]] + got1((0, 1, p, 0))
        low = held[place[0, 0, p, 1]] + got2((0, 1, p, 1))
        for dy in range(1, tall):
            top = top + got2((dy, 0, p, 0))
            low = low + got1((dy, 0, p, 1))
        both = jnp.concatenate(split(jnp.concatenate([top, low], axis=0)), axis=1)
        outer = dot(both, both, ((0,), (0,)))
        mean = (outer[:rank, :LANES] + outer[:rank, LANES:] + outer[LANES : LANES + rank, :LANES]) * (1.0 / seq)
        gsend[p] = mean.reshape(stores, rows_i, LANES)
        for d in range(1, stores):
            ship_a(p, d).start()
        graw[p, s, w] = gsend[p, s]

    def gather(p):
        for d in range(1, stores):
            ship_a(p, d).wait_recv()
        for d in range(1, wide):
            ship_b(p, d).start()

    by_rows = count % (8 * stores) == 0
    block, coords = pp.shape[2], pp.shape[3]

    def ship_r(p, d):
        peer = (s + d) % stores
        return remote(pp.at[p, peer], prs.at[p, d], sr.at[p, d], rr.at[p, d], "store", peer)

    def ship_g(p, d):
        return remote(pred.at[p], pfull.at[p, s], sg.at[p, d], rg.at[p, d], "store", (s + d) % stores)

    def condition(p):
        for d in range(1, wide):
            ship_b(p, d).wait_recv()
        got = graw[p].reshape(count, rows_i, LANES)
        lane = lax.broadcasted_iota(jnp.int32, (count, LANES), 1)
        pairs = [jnp.where(lane < rank, pltpu.roll(got[:, i, :], rank, 1), got[:, i + 1, :]) for i in range(0, rows_i, 2)]
        left = jnp.concatenate(split(jnp.concatenate(pairs, axis=1)), axis=0)
        double = dot(left, fhi[...]) + dot(left, flo[...])
        partial = double[:count] + double[count:]
        for r in range(stores):
            if by_rows:
                pp[p, r] = partial[r * block : (r + 1) * block]
            else:
                pp[p, r] = partial[:, r * coords : (r + 1) * coords]
        for d in range(1, stores):
            ship_r(p, d).start()

    def combine(p):
        total = pp[p, s]
        for d in range(1, stores):
            ship_r(p, d).wait_recv()
            total = total + prs[p, d]
        pred[p] = total
        pfull[p, s] = total
        for d in range(1, stores):
            ship_g(p, d).start()

    span = sto.shape[0] // COLS

    def ship_c(p, c, d):
        peer = (w + d) % wide
        return remote(scb.at[p, c, peer], rsc.at[p, c, d], sc.at[p, c, d], rc.at[p, c, d], "width", peer)

    def score(p, first, stop):
        for d in range(1, stores if first == 0 else 1):
            ship_g(p, d).wait_recv()
        precond = jnp.concatenate([pfull[p, r] for r in range(stores)], axis=0 if by_rows else 1)
        stacked = jnp.concatenate(split(precond), axis=0)
        for c in range(first, stop):
            rows = pl.ds(c * span, span)
            double = dot(shi[rows, :], stacked, ((1,), (1,))) + dot(slo[rows, :], stacked, ((1,), (1,)))
            double = double.T
            scores = double[:count] + double[count:]
            for r in range(wide):
                scb[p, c, r] = scores[r * stores : (r + 1) * stores]
            for d in range(1, wide):
                ship_c(p, c, d).start()

    def finish(p):
        for c in range(COLS):
            total = scb[p, c, w]
            for d in range(1, wide):
                ship_c(p, c, d).wait_recv()
                total = total + rsc[p, c, d]
            for i in range(stores):
                row = i * per + p
                out[row : row + 1, c * span : (c + 1) * span] = total[i : i + 1]

    load_f = pltpu.make_async_copy(fis, fraw, lsem.at[0])
    load_s = pltpu.make_async_copy(sto, sraw, lsem.at[1])

    def split_fisher():
        load_f.wait()
        fhi[...], flo[...] = split(fraw[...])

    def split_store():
        load_s.wait()
        step = sto.shape[0] // 16

        def part(i, carry):
            rows = pl.ds(pl.multiple_of(i * step, step), step)
            shi[rows, :], slo[rows, :] = split(sraw[rows, :])
            return carry

        lax.fori_loop(0, 16, part, 0)

    for p in range(per):
        if p == per - 1:
            load_f.start()
        lax.fori_loop(p * each, (p + 1) * each, project, 0)
        if p + 1 < per:
            forward(p)
    load_s.start()
    split_fisher()
    if per == 2:
        gradient(0)
        gather(0)
        forward(1)
        condition(0)
        split_store()
        gradient(1)
        combine(0)
        gather(1)
        condition(1)
        score(0, 0, COLS // 2)
        combine(1)
        score(0, COLS // 2, COLS)
        score(1, 0, COLS)
    else:
        forward(per - 1)
        split_store()
        for p in range(per):
            gradient(p)
            gather(p)
            condition(p)
            combine(p)
            score(p, 0, COLS)
    for p in range(per):
        finish(p)

    for p in range(per):
        for c in plans[p][0]:
            ship_1(c)[0].wait_send()
        for c in plans[p][1]:
            ship_2(c)[0].wait_send()
        for d in range(1, stores):
            ship_a(p, d).wait_send()
            ship_r(p, d).wait_send()
            ship_g(p, d).wait_send()
        for d in range(1, wide):
            ship_b(p, d).wait_send()
            for c in range(COLS):
                ship_c(p, c, d).wait_send()


def body(wide, stores, activations, out_grads, proj_in, proj_out, fisher_inv, grad_store):
    group, seq, width = activations.shape
    rank = proj_in.shape[1]
    per = group // wide
    half = seq // 2
    one, two, own = plan(wide // 2, 0)
    n1, n2 = len(one), len(two)
    examples, coords = grad_store.shape
    count = wide * stores
    queries = per * count
    out_rows = queries // wide
    if count % (8 * stores) == 0:
        piece = (count // stores, coords)
    else:
        piece = (count, coords // stores)
    rows_i = rank // stores
    span = examples // COLS
    dma = pltpu.SemaphoreType.DMA
    flat = (group * seq, width)
    return pl.pallas_call(
        functools.partial(kernel, (wide, stores, per, seq, rank)),
        out_shape=jax.ShapeDtypeStruct((out_rows, examples), F32),
        in_specs=[pl.BlockSpec(memory_space=pl.ANY)] * 2
        + [pl.BlockSpec(memory_space=pltpu.VMEM)] * 2
        + [pl.BlockSpec(memory_space=pl.ANY)] * 2,
        out_specs=pl.BlockSpec(memory_space=pltpu.VMEM),
        scratch_shapes=[
            pltpu.VMEM((DEPTH, half, width), BF16),
            pltpu.VMEM((DEPTH, half, width), BF16),
            pltpu.VMEM((width, LANES), BF16),
            pltpu.VMEM((width, LANES), BF16),
            pltpu.VMEM((per * (n1 + n2 + len(own)), half, LANES), F32),
            pltpu.VMEM((per * n1, half, LANES), F32),
            pltpu.VMEM((per * n2, half, LANES), F32),
            pltpu.VMEM(grad_store.shape, F32),
            pltpu.VMEM(grad_store.shape, BF16),
            pltpu.VMEM(grad_store.shape, BF16),
            pltpu.VMEM(fisher_inv.shape, F32),
            pltpu.VMEM(fisher_inv.shape, BF16),
            pltpu.VMEM(fisher_inv.shape, BF16),
            pltpu.VMEM((per, stores, rows_i, LANES), F32),
            pltpu.VMEM((per, stores, wide, rows_i, LANES), F32),
            pltpu.VMEM((per, stores, *piece), F32),
            pltpu.VMEM((per, stores, *piece), F32),
            pltpu.VMEM((per, *piece), F32),
            pltpu.VMEM((per, stores, *piece), F32),
            pltpu.VMEM((per, COLS, wide, stores, span), F32),
            pltpu.VMEM((per, COLS, wide, stores, span), F32),
            dma((2,)),
            dma((2, DEPTH)),
            dma((per * n1,)),
            dma((per * n1,)),
            dma((per * n2,)),
            dma((per * n2,)),
            dma((per, stores)),
            dma((per, stores)),
            dma((per, wide)),
            dma((per, wide)),
            dma((per, stores)),
            dma((per, stores)),
            dma((per, stores)),
            dma((per, stores)),
            dma((per, COLS, wide)),
            dma((per, COLS, wide)),
        ],
        compiler_params=pltpu.CompilerParams(collective_id=0, has_side_effects=True, vmem_limit_bytes=56 * 2**20),
        name="influence",
    )(activations.reshape(flat), out_grads.reshape(flat), proj_in.T, proj_out.T, fisher_inv, grad_store)


def solution(mesh):
    placed = (
        P("store", None, "width"),
        P("store", None, "width"),
        P("width", None),
        P("width", None),
        P("store", "width"),
        P("store", "width"),
    )
    return jax.shard_map(
        functools.partial(body, mesh.shape["width"], mesh.shape["store"]),
        mesh=mesh, in_specs=placed, out_specs=P("width", "store"), check_vma=False,
    )
```
